256 devices in a mesh: col: 64 (over y, z, core), lev: 4 (over x).
Axes of the slice: x: 4, y: 4, z: 8, core: 2. Of those that a mesh axis runs over, the one named last changes fastest.
Arguments:
- state: float32 [20, 80, 65536], P('lev', None, 'col'), may hold values from -6 to 6
- obs_col: int32 [2, 24576], replicated, may hold values from 0 to 65532, as said below
- obs_count: int32 [2, 64], P(None, 'col'), may hold values from 192 to 384, as said below
- obs_value: float32 [2, 24576], P(None, 'col'), may hold values from -7.5 to 7.5
- obs_var: float32 [2, 24576], P(None, 'col'), may hold values from 0.2 to 2
- horiz_weight: float32 [2, 4, 24576], P(None, None, 'col'), may hold values from 0.1 to 1
- vert_weight: float32 [2, 20, 24576], P(None, 'lev', 'col'), may hold values from 0.05 to 0.5
Outputs:
- analysis: float32 [20, 80, 65536], P('lev', None, 'col')
The draws below stay inside these ranges and needn't reach their ends.
Inputs may be any that keep to these rules, and one draw needn't show every extreme that they name: Slot s belongs to column block s div 384; its 4 stencil columns obs_col[b, s] to obs_col[b, s] + 3 all lie in that block. `obs_count`: in every batch some column block uses all 384 of its slots.
All inputs are finite; a program needn't handle non-finite values.
Results may differ from the reference program's by a relative error of at most 0.0003.
Values sent between devices are 32-bit elements; how exact they have to be, the bound alone decides.
A program may use at most 64 MiB of HBM per device.

```python
import math
import jax
import jax.numpy as jnp
from jax import lax

MEM = 80
LEVELS = 20
COL_DEV = 1024
NCOL = 65536
CAP = 384
SLOTS = 24576
BATCHES = 2
STENCIL = 4
RADIUS = 512


def draw_obs_col(key, part):
    key = jax.random.fold_in(key, 11)
    blocks = SLOTS // CAP
    offsets = jax.random.randint(key, (BATCHES, blocks, CAP), 0, COL_DEV - STENCIL + 1)
    starts = (jnp.arange(blocks, dtype=jnp.int32) * COL_DEV)[None, :, None]
    return (offsets + starts).reshape(BATCHES, SLOTS).astype(jnp.int32)


def draw_obs_count(key, part):
    key = jax.random.fold_in(key, 12)
    blocks = SLOTS // CAP
    drawn_key, busy_key = jax.random.split(key)
    drawn = jax.random.randint(drawn_key, (BATCHES, blocks), CAP // 2, CAP + 1)
    busiest = jax.random.randint(busy_key, (BATCHES, 1), 0, blocks)
    return jnp.where(jnp.arange(blocks, dtype=jnp.int32)[None, :] == busiest, CAP, drawn).astype(jnp.int32)


def draw_obs_value(key, part):
    key = jax.random.fold_in(key, 13)
    blocks = SLOTS // CAP
    ramp = (jnp.arange(blocks, dtype=jnp.float32) / (blocks - 1))[None, :, None]
    values = jax.random.truncated_normal(key, -4.0, 4.0, (BATCHES, blocks, CAP), jnp.float32) * 0.6 * (1.0 + 2.0 * ramp)
    return values.reshape(BATCHES, SLOTS).astype(jnp.float32)


def block_scale(rng, dims, shards, smallest, top_value):
    def one(axis_at, shards_of):
        draws = jax.random.uniform(jax.random.fold_in(jax.random.fold_in(rng, 6), axis_at), (shards_of,), jnp.float32, smallest / len(shards), top_value / len(shards))
        return jnp.repeat(jnp.exp(draws), dims[axis_at] // shards_of).reshape((-1,) + (1,) * (len(dims) - axis_at - 1))

    level = one(*shards[0])
    for cut in shards[1:]:
        level = level * one(*cut)
    return level


def bell_draw(rng, shape, scale, bound, shards=(), kind=jnp.bfloat16):
    gain = block_scale(rng, shape, shards, -0.22, 0.18) if shards else 1.0
    drawn = jax.random.normal(rng, shape, jnp.float32) * scale * gain
    return jnp.minimum(jnp.maximum(drawn, -bound), bound).astype(kind)


def setup_inputs(seed: int = 0) -> dict:
    streams_of = jax.random.split(jax.random.key(seed), 8)
    state = bell_draw(streams_of[0], (LEVELS, MEM, NCOL), 1.0, 6.0, ((0, 4), (2, 64)), jnp.float32)
    obs_col = draw_obs_col(jax.random.fold_in(streams_of[7], 71), 0)
    obs_count = draw_obs_count(jax.random.fold_in(streams_of[7], 71), 0)
    obs_value = draw_obs_value(jax.random.fold_in(streams_of[7], 71), 0)
    obs_var = jnp.clip(jnp.exp(math.log(2.0) - 2.3025851 * jax.random.uniform(streams_of[4], (BATCHES, SLOTS), jnp.float32) ** block_scale(streams_of[4], (BATCHES, SLOTS), ((1, 64),), -0.2, 0.2)), 0.2, 2.0)
    horiz_weight = jnp.clip(0.1 + 0.9 * jax.random.uniform(streams_of[5], (BATCHES, STENCIL, SLOTS), jnp.float32) ** block_scale(streams_of[5], (BATCHES, STENCIL, SLOTS), ((2, 64),), -0.2, 0.2), 0.1, 1.0)
    vert_weight = jnp.clip(jnp.exp(math.log(0.5) - 2.3025851 * jax.random.uniform(streams_of[6], (BATCHES, LEVELS, SLOTS), jnp.float32) ** block_scale(streams_of[6], (BATCHES, LEVELS, SLOTS), ((1, 4), (2, 64)), -0.2, 0.2)), 0.05, 0.5)
    return dict(state=state, obs_col=obs_col, obs_count=obs_count, obs_value=obs_value, obs_var=obs_var, horiz_weight=horiz_weight, vert_weight=vert_weight)


epsilon = 1e-06

def gc_taper(distance, half_width):
    ratio = distance / half_width
    near_part = (((-0.25 * ratio + 0.5) * ratio + 0.625) * ratio - 5.0 / 3.0) * ratio * ratio + 1.0
    ratio_safe = jnp.maximum(ratio, 1.0)
    far_part = ((((ratio_safe / 12.0 - 0.5) * ratio_safe + 0.625) * ratio_safe + 5.0 / 3.0) * ratio_safe - 5.0) * ratio_safe + 4.0 - 2.0 / (3.0 * ratio_safe)
    return jnp.where(ratio <= 1.0, near_part, jnp.where(ratio < 2.0, far_part, 0.0 * ratio))

def cycle_taper(obs_cols, columns, cycle_len, reach):
    gap = jnp.mod(obs_cols[:, None] - columns[None, :], cycle_len)
    distance = jnp.minimum(gap, cycle_len - gap).astype(jnp.float32)
    return gc_taper(distance, reach / 2.0)

def increments(obs_anom, innovation, prior_var, noise, inflation, members):
    inflated_var = inflation * prior_var
    mean_shift = inflated_var * innovation / (inflated_var + noise)
    shrink = jnp.sqrt(noise / (inflated_var + noise)) - 1.0
    obs_shift = mean_shift[None, :] + shrink[None, :] * jnp.sqrt(inflation) * obs_anom
    regress = obs_anom / ((members - 1) * (prior_var + epsilon))[None, :]
    return (obs_shift, regress)

def reference(state, obs_col, obs_count, obs_value, obs_var, horiz_weight, vert_weight):
    blocks = SLOTS // CAP
    current = state
    for which_batch in range(BATCHES):
        obs_cols = obs_col[which_batch]
        obs_prior = jnp.zeros((MEM, SLOTS), jnp.float32)
        for shift_idx in range(STENCIL):
            picked = jnp.take(current, obs_cols + shift_idx, axis=2)
            level_mix = jnp.einsum('lms,ls->ms', picked, vert_weight[which_batch], precision=lax.Precision.HIGHEST)
            obs_prior = obs_prior + level_mix * horiz_weight[which_batch, shift_idx][None, :]
        in_use = (jnp.arange(CAP, dtype=jnp.int32)[None, :] < obs_count[which_batch][:, None]).reshape(SLOTS).astype(jnp.float32)
        obs_mean = lax.optimization_barrier(jnp.mean(obs_prior, axis=0))
        deviation = obs_prior - obs_mean[None, :]
        prior_var = lax.optimization_barrier(jnp.sum(deviation * deviation, axis=0)) / (MEM - 1)
        obs_anom = deviation * in_use[None, :]
        innovation = (obs_value[which_batch] - obs_mean) * in_use
        noise = obs_var[which_batch]
        misfit = jnp.sum(innovation * innovation)
        expected = jnp.sum(in_use * (prior_var + noise))
        inflation = misfit / expected
        obs_shift, regress = increments(obs_anom, innovation, prior_var, noise, inflation, MEM)
        shift_blocks = obs_shift.reshape(MEM, blocks, CAP)
        regress_blocks = regress.reshape(MEM, blocks, CAP)
        col_blocks = obs_cols.reshape(blocks, CAP)
        centre = lax.optimization_barrier(jnp.mean(current, axis=1, keepdims=True))

        def one_block(block_no):
            nearby = jnp.mod(block_no + jnp.arange(3, dtype=jnp.int32) - 1, blocks).astype(jnp.int32)
            near_shift = jnp.take(shift_blocks, nearby, axis=1).reshape(MEM, 3 * CAP)
            near_regress = jnp.take(regress_blocks, nearby, axis=1).reshape(MEM, 3 * CAP)
            near_cols = jnp.take(col_blocks, nearby, axis=0).reshape(3 * CAP)
            first_col = (block_no * COL_DEV).astype(jnp.int32)
            columns = first_col + jnp.arange(COL_DEV, dtype=jnp.int32)
            loc_weight = cycle_taper(near_cols, columns, NCOL, RADIUS)
            block_state = lax.dynamic_slice_in_dim(current, first_col, COL_DEV, 2)
            block_centre = lax.dynamic_slice_in_dim(centre, first_col, COL_DEV, 2)
            spread = block_state - block_centre
            inflated = block_centre + jnp.sqrt(inflation) * spread

            def one_level(pair):
                level_spread, level_inflated = pair
                coefs = lax.dot_general(near_regress, level_spread, (((0,), (0,)), ((), ())), precision=lax.Precision.HIGHEST)
                return level_inflated + jnp.dot(near_shift, loc_weight * coefs, precision=lax.Precision.HIGHEST)
            return lax.map(one_level, (spread, inflated))
        updated = lax.map(one_block, jnp.arange(blocks, dtype=jnp.int32))
        current = jnp.transpose(updated, (1, 2, 0, 3)).reshape(LEVELS, MEM, NCOL)
    return current
```

```python
import functools
import jax
import jax.numpy as jnp
from jax import lax
from jax.experimental import pallas as pl
from jax.experimental.pallas import tpu as pltpu
from jax.sharding import PartitionSpec as P

MESH = pl.DeviceIdType.MESH
F32 = jnp.float32
BF16 = jnp.bfloat16

BATCHES = 2
LEV = 5
MEM = 80
COLS = 1024
CAP = 384
QUART = 96
LANES = 128
HALF = 512
NZ = 8
NY = 4
NLEV = 4
EPS = 1e-06


def split(x):
    hi = x.astype(BF16)
    return hi, (x - hi.astype(F32)).astype(BF16)


def pad_quarters(x):
    return [
        (x if q == 0 else pltpu.roll(x, CAP - QUART * q, 1))[:, :LANES]
        for q in range(4)
    ]


def pack_quarters(q0, q1, q2, q3):
    lane = lax.broadcasted_iota(jnp.int32, q0.shape, 1)
    r1 = pltpu.roll(q1, 96, 1)
    r2 = pltpu.roll(q2, 64, 1)
    r3 = pltpu.roll(q3, 32, 1)
    return jnp.concatenate(
        [
            jnp.where(lane < 96, q0, r1),
            jnp.where(lane < 64, r1, r2),
            jnp.where(lane < 32, r2, r3),
        ],
        axis=1,
    )


def taper(dist):
    r = dist * (1.0 / 256.0)
    near = (((-0.25 * r + 0.5) * r + 0.625) * r - 5.0 / 3.0) * (r * r) + 1.0
    t = jnp.maximum(2.0 - r, 0.0)
    t2 = t * t
    rs = jnp.maximum(r, 1.0)
    far = (t2 * t2) * ((rs + 2.0) * rs - 0.5) * pl.reciprocal(12.0 * rs)
    return jnp.where(r <= 1.0, near, far)


def remote(src, dst, send, recv, dev):
    return pltpu.make_async_remote_copy(
        src_ref=src, dst_ref=dst, send_sem=send, recv_sem=recv,
        device_id=dev, device_id_type=MESH,
    )


def kernel(
    state, obs_col, obs_count, obs_value, obs_var, hw, vw, out,
    X, CEN, SPC, XHL, HH, HL, LOC, PT, RT, SC, ZH, ZL, MV, META, PART, RSB, PRI, G1, G2,
    dma_sem, meta_s, meta_r, rs_s, rs_r, ag_s, ag_r, ha_s, ha_r, g1_s, g1_r, g2_s, g2_r,
):
    i = lax.axis_index("col")
    j = lax.axis_index("lev")
    core = lax.rem(i, 2)
    z = lax.rem(i // 2, NZ)
    y = i // (2 * NZ)
    left = lax.rem(i + 63, 64)
    right = lax.rem(i + 1, 64)
    lev_peers = [lax.rem(j + d, NLEV) for d in range(NLEV)]
    g1_peers = [
        {"col": lax.rem(y + dy, NY) * 16 + z * 2 + core, "lev": lax.rem(j + dl, NLEV)}
        for dl in range(NLEV) for dy in range(NY) if dl or dy
    ]
    g2_peers = [
        {"col": y * 16 + lax.rem(z + dz, NZ) * 2 + lax.rem(core + dc, 2), "lev": j}
        for dz in range(NZ) for dc in range(2) if dz or dc
    ]
    g1_me = j * NY + y
    g2_me = z * 2 + core

    barrier = pltpu.get_barrier_semaphore()
    partners = g1_peers + g2_peers + [{"col": left, "lev": j}, {"col": right, "lev": j}]
    for dev in partners:
        pl.semaphore_signal(barrier, inc=1, device_id=dev, device_id_type=MESH)
    load = pltpu.make_async_copy(state, X, dma_sem)
    load.start()

    starts = [obs_col[:, pl.ds(pl.multiple_of(b * CAP, CAP), CAP)] for b in (i, left, right)]
    lane384 = lax.broadcasted_iota(jnp.int32, (1, CAP), 1)
    use = [(lane384 < obs_count[b, 0]).astype(F32) for b in range(BATCHES)]
    META[0] = jnp.concatenate(
        [obs_value[...], obs_var[...], use[0], use[1], jnp.zeros((2, CAP), F32)], axis=0
    )
    MV[...] = jnp.stack(pad_quarters(META[0]))
    rel = [
        (starts[0] - i * COLS).astype(F32),
        (starts[1] - left * COLS - COLS).astype(F32),
        (starts[2] - right * COLS + COLS).astype(F32),
    ]
    PT[...] = jnp.concatenate(rel + [jnp.zeros((LANES - 6, CAP), F32)], axis=0).T

    def build_gather(b):
        lane = lax.broadcasted_iota(jnp.int32, (1, LANES), 1)
        valid = lane < QUART
        st = pad_quarters(starts[0] - i * COLS)
        h4 = pad_quarters(hw[b])
        start = jnp.concatenate([s[b : b + 1] for s in st], axis=1)
        w = jnp.concatenate([jnp.where(valid, h, 0.0) for h in h4], axis=1)

        @pl.loop(0, COLS // 32)
        def _(k):
            rows = pl.ds(pl.multiple_of(k * 32, 32), 32)
            t = lax.broadcasted_iota(jnp.int32, (32, 4 * LANES), 0) + (k * 32 - start)
            m = jnp.zeros((32, 4 * LANES), F32)
            for n in range(4):
                m = jnp.where(t == n, w[n : n + 1], m)
            HH[b, rows, :], HL[b, rows, :] = split(m)

    def build_taper(b):
        for half in range(2):
            for grp in range(2):
                blk = 0 if grp == 0 else 1 + half

                @pl.loop(0, CAP // 32)
                def _(k):
                    rows = pl.ds(pl.multiple_of(k * 32, 32), 32)
                    p = PT[rows, 2 * blk + b : 2 * blk + b + 1]
                    c = (lax.broadcasted_iota(jnp.int32, (32, HALF), 1) + half * HALF).astype(F32)
                    LOC[b, half, grp, rows, :] = taper(jnp.abs(p - c))

    def partial_priors(b):
        @pl.loop(0, LEV)
        def _(l):
            x = X[l]
            hi, lo = split(x)
            XHL[pl.ds(pl.multiple_of(l * MEM, MEM), MEM), :] = hi
            XHL[pl.ds(pl.multiple_of(LEV * MEM + l * MEM, MEM), MEM), :] = lo

        v4 = pad_quarters(vw[b])
        for n in range(2):
            cols = slice(n * 256, n * 256 + 256)
            a = jnp.dot(XHL[...], HH[b, :, cols], preferred_element_type=F32)
            r = jnp.dot(XHL[: LEV * MEM], HL[b, :, cols], preferred_element_type=F32)
            v = jnp.concatenate([v4[2 * n], v4[2 * n + 1]], axis=1)
            total = None
            for l in range(LEV):
                term = a[l * MEM : (l + 1) * MEM] + a[(LEV + l) * MEM : (LEV + l + 1) * MEM]
                term = (term + r[l * MEM : (l + 1) * MEM]) * v[l : l + 1]
                total = term if total is None else total + term
            PART[b, 2 * n] = total[:, :LANES]
            PART[b, 2 * n + 1] = total[:, LANES:]

    def prepare_spread():
        @pl.loop(0, LEV)
        def _(l):
            x = X[l]
            centre = jnp.mean(x, axis=0, keepdims=True)
            CEN[l] = jnp.broadcast_to(centre, (8, COLS))
            hi, lo = split(x - centre)
            SPC[l, 0:MEM] = hi
            SPC[l, MEM : 2 * MEM] = hi
            SPC[l, 2 * MEM : 3 * MEM] = lo
            SPC[l, 3 * MEM :] = jnp.zeros((16, COLS), BF16)

    def stats(prior):
        mean = jnp.sum(prior, axis=0, keepdims=True) / MEM
        dev = prior - mean
        var = jnp.sum(dev * dev, axis=0, keepdims=True) / (MEM - 1)
        return mean, dev, var

    build_gather(0)
    load.wait()
    partial_priors(0)
    pl.semaphore_wait(barrier, len(partners))

    meta_copies = [
        remote(META.at[0], META.at[1], meta_s.at[0], meta_r.at[0], {"col": right, "lev": j}),
        remote(META.at[0], META.at[2], meta_s.at[1], meta_r.at[1], {"col": left, "lev": j}),
    ]
    pending = []

    for b in range(BATCHES):
        copies = []
        for d in (2, 1, 3):
            c = remote(PART.at[b, lev_peers[d]], RSB.at[b, d - 1], rs_s.at[b, d - 1], rs_r.at[b, d - 1],
                       {"col": i, "lev": lev_peers[d]})
            c.start()
            copies.append(c)
        if b == 0:
            for c in meta_copies:
                c.start()
            build_taper(0)
        prepare_spread()
        for c in copies:
            c.wait_recv()
        pending += copies
        prior = PART[b, j] + (RSB[b, 0] + RSB[b, 1] + RSB[b, 2])
        PRI[b, 0, j] = prior

        def forward(q):
            made = [
                remote(PRI.at[b, 0, q], PRI.at[b, 1, q], ha_s.at[b, 0, q], ha_r.at[b, 0, q],
                       {"col": right, "lev": j}),
                remote(PRI.at[b, 0, q], PRI.at[b, 2, q], ha_s.at[b, 1, q], ha_r.at[b, 1, q],
                       {"col": left, "lev": j}),
            ]
            for c in made:
                c.start()
            pending.extend(made)

        gathers = []
        for d in (2, 1, 3):
            c = remote(PRI.at[b, 0, j], PRI.at[b, 0, j], ag_s.at[b, d - 1], ag_r.at[b, d - 1],
                       {"col": i, "lev": lev_peers[d]})
            c.start()
            gathers.append((d, c))
        forward(j)

        mean, dev, var = stats(prior)
        lane = lax.broadcasted_iota(jnp.int32, (1, LANES), 1)
        value = MV[j, b : b + 1]
        noise = MV[j, 2 + b : 3 + b]
        used = jnp.where(lane < QUART, MV[j, 4 + b : 5 + b], 0.0)
        innov = (value - mean) * used
        misfit = jnp.sum(innov * innov, axis=1, keepdims=True)
        expected = jnp.sum(used * (var + noise), axis=1, keepdims=True)
        G1[b, pl.ds(g1_me, 1), :] = jnp.where(lane < 64, misfit, expected)
        for dev_id in g1_peers:
            row = G1.at[b, pl.ds(g1_me, 1)]
            remote(row, row, g1_s.at[b], g1_r.at[b], dev_id).start()
        if b == 0:
            build_gather(1)
        for d, c in gathers:
            c.wait_recv()
            forward(lax.rem(j + NLEV - d, NLEV))
        pending += [c for _, c in gathers]

        all15 = G1.at[b, pl.ds(0, 15)]
        remote(all15, all15, g1_s.at[b], g1_r.at[b], g1_peers[0]).wait()
        G2[b, pl.ds(g2_me, 1), :] = jnp.sum(G1[b], axis=0, keepdims=True)
        for dev_id in g2_peers:
            row = G2.at[b, pl.ds(g2_me, 1)]
            remote(row, row, g2_s.at[b], g2_r.at[b], dev_id).start()

        kept = []

        def regression(blk):
            prior3 = pack_quarters(*[PRI[b, blk, q] for q in range(4)])
            mean, dev, var = stats(prior3)
            used = META[blk, 4 + b : 5 + b]
            anom = dev * used
            innov = (META[blk, b : b + 1] - mean) * used
            kept.append((anom, innov, var))
            regress = anom / ((MEM - 1) * (var + EPS))
            hi = regress.astype(BF16).astype(F32)
            lo = regress - hi
            for t in range(3):
                cut = slice(t * LANES, (t + 1) * LANES)
                tall = jnp.concatenate([hi[:, cut], lo[:, cut], hi[:, cut], jnp.zeros((16, LANES), F32)], axis=0)
                RT[blk, cut, :] = tall.T.astype(BF16)

        def first_product(grp):
            @pl.loop(0, LEV)
            def _(l):
                for c4 in range(4):
                    half, ct = c4 // 2, c4 % 2
                    blk = 0 if grp == 0 else 1 + half
                    cols = slice(c4 * 256, c4 * 256 + 256)
                    coef = jnp.dot(RT[blk], SPC[l, :, cols], preferred_element_type=F32)
                    hi, lo = split(coef * LOC[b, half, grp, :, ct * 256 : ct * 256 + 256])
                    ZH[l, grp * CAP : (grp + 1) * CAP, cols] = hi
                    ZL[l, grp * CAP : (grp + 1) * CAP, cols] = lo

        regression(0)
        first_product(0)
        if b == 0:
            for c in meta_copies:
                c.wait()
            build_taper(1)
        for side in range(2):
            for q in range(4):
                remote(PRI.at[b, 0, q], PRI.at[b, 1 + side, q], ha_s.at[b, side, q], ha_r.at[b, side, q],
                       {"col": right, "lev": j}).wait_recv()
        regression(1)
        regression(2)
        first_product(1)

        all15 = G2.at[b, pl.ds(0, 15)]
        remote(all15, all15, g2_s.at[b], g2_r.at[b], g2_peers[0]).wait()
        sums = jnp.sum(G2[b], axis=0, keepdims=True)
        inflation = sums[:, 0:1] / sums[:, 64:65]
        root = jnp.sqrt(inflation)
        for blk in range(3):
            anom, innov, var = kept[blk]
            noise = META[blk, 2 + b : 3 + b]
            v = inflation * var
            tot = v + noise
            shift = v * innov / tot + ((jnp.sqrt(noise / tot) - 1.0) * root) * anom
            hi, lo = split(shift)
            cut = slice(0, CAP) if blk == 0 else slice(CAP, 2 * CAP)
            for half in ((0, 1) if blk == 0 else (blk - 1,)):
                SC[half, 0:MEM, cut] = hi
                SC[half, MEM : 2 * MEM, cut] = lo

        target = X if b + 1 < BATCHES else out

        @pl.loop(0, LEV)
        def _(l):
            for c4 in range(4):
                half = c4 // 2
                cols = slice(c4 * 256, c4 * 256 + 256)
                a = jnp.dot(SC[half], ZH[l, :, cols], preferred_element_type=F32)
                r = jnp.dot(SC[half, 0:MEM], ZL[l, :, cols], preferred_element_type=F32)
                centre = CEN[l, 0:1, cols]
                base = centre + root * (X[l, :, cols] - centre)
                target[l, :, cols] = base + (a[:MEM] + a[MEM:] + r)

        if b + 1 < BATCHES:
            partial_priors(b + 1)

    for c in pending:
        c.wait_send()


def shards(state, obs_col, obs_count, obs_value, obs_var, horiz_weight, vert_weight):
    vm = pl.BlockSpec(memory_space=pltpu.VMEM)
    dma = pltpu.SemaphoreType.DMA
    return pl.pallas_call(
        kernel,
        name="window",
        out_shape=jax.ShapeDtypeStruct((LEV, MEM, COLS), F32),
        in_specs=[pl.BlockSpec(memory_space=pl.ANY), vm, pl.BlockSpec(memory_space=pltpu.SMEM), vm, vm, vm, vm],
        out_specs=vm,
        scratch_shapes=[
            pltpu.VMEM((LEV, MEM, COLS), F32),
            pltpu.VMEM((LEV, 8, COLS), F32),
            pltpu.VMEM((LEV, 256, COLS), BF16),
            pltpu.VMEM((2 * LEV * MEM, COLS), BF16),
            pltpu.VMEM((BATCHES, COLS, 4 * LANES), BF16),
            pltpu.VMEM((BATCHES, COLS, 4 * LANES), BF16),
            pltpu.VMEM((BATCHES, 2, 2, CAP, HALF), F32),
            pltpu.VMEM((CAP, LANES), F32),
            pltpu.VMEM((3, CAP, 256), BF16),
            pltpu.VMEM((2, 2 * MEM, 2 * CAP), BF16),
            pltpu.VMEM((LEV, 2 * CAP, COLS), BF16),
            pltpu.VMEM((LEV, 2 * CAP, COLS), BF16),
            pltpu.VMEM((4, 8, LANES), F32),
            pltpu.VMEM((3, 8, CAP), F32),
            pltpu.VMEM((BATCHES, 4, MEM, LANES), F32),
            pltpu.VMEM((BATCHES, 3, MEM, LANES), F32),
            pltpu.VMEM((BATCHES, 3, 4, MEM, LANES), F32),
            pltpu.VMEM((BATCHES, 16, LANES), F32),
            pltpu.VMEM((BATCHES, 16, LANES), F32),
            dma,
            dma((2,)), dma((2,)),
            dma((BATCHES, 3)), dma((BATCHES, 3)),
            dma((BATCHES, 3)), dma((BATCHES, 3)),
            dma((BATCHES, 2, 4)), dma((BATCHES, 2, 4)),
            dma((BATCHES,)), dma((BATCHES,)),
            dma((BATCHES,)), dma((BATCHES,)),
        ],
        compiler_params=pltpu.CompilerParams(
            collective_id=0, has_side_effects=True, vmem_limit_bytes=56 * 1024 * 1024
        ),
    )(state, obs_col, obs_count, obs_value, obs_var, horiz_weight, vert_weight)


def solution(mesh):
    placed = (
        P("lev", None, "col"),
        P(),
        P(None, "col"),
        P(None, "col"),
        P(None, "col"),
        P(None, None, "col"),
        P(None, "lev", "col"),
    )
    return jax.shard_map(
        shards, mesh=mesh, in_specs=placed, out_specs=P("lev", None, "col"), check_vma=False
    )
```

```python
import functools
import jax
import jax.numpy as jnp
from jax import lax
from jax.experimental import pallas as pl
from jax.experimental.pallas import tpu as pltpu
from jax.sharding import PartitionSpec as P

MESH = pl.DeviceIdType.MESH
F32 = jnp.float32
BF16 = jnp.bfloat16

BATCHES = 2
LEV = 5
MEM = 80
COLS = 1024
CAP = 384
QUART = 96
LANES = 128
HALF = 512
NZ = 8
NY = 4
NLEV = 4
EPS = 1e-06


def split(x):
    hi = x.astype(BF16)
    return hi, (x - hi.astype(F32)).astype(BF16)


def pad_quarters(x):
    return [
        (x if q == 0 else pltpu.roll(x, CAP - QUART * q, 1))[:, :LANES]
        for q in range(4)
    ]


def pack_quarters(q0, q1, q2, q3):
    lane = lax.broadcasted_iota(jnp.int32, q0.shape, 1)
    r1 = pltpu.roll(q1, 96, 1)
    r2 = pltpu.roll(q2, 64, 1)
    r3 = pltpu.roll(q3, 32, 1)
    return jnp.concatenate(
        [
            jnp.where(lane < 96, q0, r1),
            jnp.where(lane < 64, r1, r2),
            jnp.where(lane < 32, r2, r3),
        ],
        axis=1,
    )


def taper(d):
    u = 1.0 / 256.0
    near = ((-0.25 * u**5) * d + 0.5 * u**4) * d + 0.625 * u**3
    near = (near * d - (5.0 / 3.0) * u**2) * (d * d) + 1.0
    t = jnp.maximum(512.0 - d, 0.0)
    t2 = t * t
    far = (t2 * t2) * ((u**5 / 12.0) * d + u**4 / 6.0 - (u**3 / 24.0) * pl.reciprocal(d))
    return jnp.where(d <= 256.0, near, far)


def remote(src, dst, send, recv, dev):
    return pltpu.make_async_remote_copy(
        src_ref=src, dst_ref=dst, send_sem=send, recv_sem=recv,
        device_id=dev, device_id_type=MESH,
    )


def kernel(
    state, obs_col, obs_count, obs_value, obs_var, hw_in, vw_in, out,
    OCOL, OCNT, OVAL, OVAR, hw, vw, OUT, X, CEN, SPC, XHL, HH, HL, LOC, PT, RT, SC, ZH, ZL, MV, META, PART, RSB, PRI, G1, G2,
    in_sem, out_sem, meta_s, meta_r, rs_s, rs_r, ag_s, ag_r, ha_s, ha_r, g1_s, g1_r, g2_s, g2_r,
):
    i = lax.axis_index("col")
    j = lax.axis_index("lev")
    core = lax.rem(i, 2)
    z = lax.rem(i // 2, NZ)
    y = i // (2 * NZ)
    left = lax.rem(i + 63, 64)
    right = lax.rem(i + 1, 64)
    lev_peers = [lax.rem(j + d, NLEV) for d in range(NLEV)]
    g1_peers = [
        {"col": lax.rem(y + dy, NY) * 16 + z * 2 + core, "lev": lax.rem(j + dl, NLEV)}
        for dl in (2, 1, 3, 0) for dy in (2, 1, 3, 0) if dl or dy
    ]
    g2_peers = [
        {"col": y * 16 + lax.rem(z + dz, NZ) * 2 + lax.rem(core + dc, 2), "lev": j}
        for dz in (4, 3, 5, 2, 6, 1, 7, 0) for dc in (1, 0) if dz or dc
    ]
    g1_me = j * NY + y
    g2_me = z * 2 + core

    blocks = (i, left, right)
    loads = [
        pltpu.make_async_copy(obs_col.at[:, pl.ds(pl.multiple_of(b * CAP, CAP), CAP)], OCOL.at[n], in_sem.at[n])
        for n, b in enumerate(blocks)
    ]
    for n, (src, dst) in enumerate(
        ((obs_count, OCNT), (obs_value, OVAL), (obs_var, OVAR), (hw_in, hw), (vw_in, vw))
    ):
        loads.append(pltpu.make_async_copy(src, dst, in_sem.at[3 + n]))
    load_state = pltpu.make_async_copy(state, X, in_sem.at[8])
    for c in loads + [load_state]:
        c.start()
    barrier = pltpu.get_barrier_semaphore()
    partners = g1_peers + g2_peers + [{"col": left, "lev": j}, {"col": right, "lev": j}]
    for dev in partners:
        pl.semaphore_signal(barrier, inc=1, device_id=dev, device_id_type=MESH)
    for c in loads:
        c.wait()

    starts = [OCOL[n] for n in range(3)]
    lane384 = lax.broadcasted_iota(jnp.int32, (1, CAP), 1)
    use = [(lane384 < OCNT[0:1, b : b + 1]).astype(F32) for b in range(BATCHES)]
    META[0] = jnp.concatenate(
        [OVAL[...], OVAR[...], use[0], use[1], jnp.zeros((2, CAP), F32)], axis=0
    )
    MV[...] = jnp.stack(pad_quarters(META[0]))
    rel = [
        (starts[0] - i * COLS).astype(F32),
        (starts[1] - left * COLS - COLS).astype(F32),
        (starts[2] - right * COLS + COLS).astype(F32),
    ]
    PT[...] = jnp.concatenate(rel + [jnp.zeros((LANES - 6, CAP), F32)], axis=0).T

    def build_gather(b):
        lane = lax.broadcasted_iota(jnp.int32, (1, LANES), 1)
        valid = lane < QUART
        st = pad_quarters(starts[0] - i * COLS)
        h4 = pad_quarters(hw[b])
        start = jnp.concatenate([s[b : b + 1] for s in st], axis=1)
        w = jnp.concatenate([jnp.where(valid, h, 0.0) for h in h4], axis=1)

        @pl.loop(0, COLS // 32)
        def _(k):
            rows = pl.ds(pl.multiple_of(k * 32, 32), 32)
            t = lax.broadcasted_iota(jnp.int32, (32, 4 * LANES), 0) + (k * 32 - start)
            m = jnp.zeros((32, 4 * LANES), F32)
            for n in range(4):
                m = jnp.where(t == n, w[n : n + 1], m)
            HH[b, rows, :], HL[b, rows, :] = split(m)

    def build_taper(b, grp):
        for half in range(2):
            blk = 0 if grp == 0 else 1 + half

            @pl.loop(0, CAP // 192)
            def _(k):
                rows = pl.ds(pl.multiple_of(k * 192, 192), 192)
                p = PT[rows, 2 * blk + b : 2 * blk + b + 1]
                c = (lax.broadcasted_iota(jnp.int32, (192, HALF), 1) + half * HALF).astype(F32)
                LOC[half, grp, rows, :] = taper(jnp.abs(p - c))

    def partial_priors(b):
        @pl.loop(0, LEV)
        def _(l):
            x = X[l]
            hi, lo = split(x)
            XHL[pl.ds(pl.multiple_of(l * MEM, MEM), MEM), :] = hi
            XHL[pl.ds(pl.multiple_of(LEV * MEM + l * MEM, MEM), MEM), :] = lo

        v4 = pad_quarters(vw[:, b, :])
        for n in range(2):
            cols = slice(n * 256, n * 256 + 256)
            a = jnp.dot(XHL[...], HH[b, :, cols], preferred_element_type=F32)
            r = jnp.dot(XHL[: LEV * MEM], HL[b, :, cols], preferred_element_type=F32)
            v = jnp.concatenate([v4[2 * n], v4[2 * n + 1]], axis=1)
            total = None
            for l in range(LEV):
                term = a[l * MEM : (l + 1) * MEM] + a[(LEV + l) * MEM : (LEV + l + 1) * MEM]
                term = (term + r[l * MEM : (l + 1) * MEM]) * v[l : l + 1]
                total = term if total is None else total + term
            PART[b, 2 * n] = total[:, :LANES]
            PART[b, 2 * n + 1] = total[:, LANES:]

    def prepare_spread():
        @pl.loop(0, LEV)
        def _(l):
            x = X[l]
            centre = jnp.mean(x, axis=0, keepdims=True)
            CEN[l] = jnp.broadcast_to(centre, (8, COLS))
            hi, lo = split(x - centre)
            SPC[l, 0:MEM] = hi
            SPC[l, MEM : 2 * MEM] = hi
            SPC[l, 2 * MEM : 3 * MEM] = lo
            SPC[l, 3 * MEM :] = jnp.zeros((16, COLS), BF16)

    def stats(prior):
        mean = jnp.sum(prior, axis=0, keepdims=True) / MEM
        dev = prior - mean
        var = jnp.sum(dev * dev, axis=0, keepdims=True) / (MEM - 1)
        return mean, dev, var

    build_gather(0)
    load_state.wait()
    partial_priors(0)
    pl.semaphore_wait(barrier, len(partners))

    meta_copies = [
        remote(META.at[0], META.at[1], meta_s.at[0], meta_r.at[0], {"col": right, "lev": j}),
        remote(META.at[0], META.at[2], meta_s.at[1], meta_r.at[1], {"col": left, "lev": j}),
    ]
    pending, stores = [], []

    for b in range(BATCHES):
        copies = []
        for d in (2, 1, 3):
            c = remote(PART.at[b, lev_peers[d]], RSB.at[b, d - 1], rs_s.at[b, d - 1], rs_r.at[b, d - 1],
                       {"col": i, "lev": lev_peers[d]})
            c.start()
            copies.append(c)
        if b == 0:
            for c in meta_copies:
                c.start()
        build_taper(b, 0)
        prepare_spread()
        for c in copies:
            c.wait_recv()
        pending += copies
        prior = PART[b, j] + (RSB[b, 0] + RSB[b, 1] + RSB[b, 2])
        PRI[b, 0, j] = prior

        mean, dev, var = stats(prior)
        lane = lax.broadcasted_iota(jnp.int32, (1, LANES), 1)
        value = MV[j, b : b + 1]
        noise = MV[j, 2 + b : 3 + b]
        used = jnp.where(lane < QUART, MV[j, 4 + b : 5 + b], 0.0)
        innov = (value - mean) * used
        misfit = jnp.sum(innov * innov, axis=1, keepdims=True)
        expected = jnp.sum(used * (var + noise), axis=1, keepdims=True)
        G1[b, pl.ds(g1_me, 1), :] = jnp.where(lane < 64, misfit, expected)
        for dev_id in g1_peers:
            row = G1.at[b, pl.ds(g1_me, 1)]
            remote(row, row, g1_s.at[b], g1_r.at[b], dev_id).start()
        def forward(q):
            made = [
                remote(PRI.at[b, 0, q], PRI.at[b, 1, q], ha_s.at[b, 0, q], ha_r.at[b, 0, q],
                       {"col": right, "lev": j}),
                remote(PRI.at[b, 0, q], PRI.at[b, 2, q], ha_s.at[b, 1, q], ha_r.at[b, 1, q],
                       {"col": left, "lev": j}),
            ]
            for c in made:
                c.start()
            pending.extend(made)

        gathers = []
        for d in (2, 1, 3):
            c = remote(PRI.at[b, 0, j], PRI.at[b, 0, j], ag_s.at[b, d - 1], ag_r.at[b, d - 1],
                       {"col": i, "lev": lev_peers[d]})
            c.start()
            gathers.append((d, c))
        forward(j)
        build_taper(b, 1)
        for d, c in gathers:
            c.wait_recv()
            forward(lax.rem(j + NLEV - d, NLEV))
        pending += [c for _, c in gathers]

        all15 = G1.at[b, pl.ds(0, 15)]
        remote(all15, all15, g1_s.at[b], g1_r.at[b], g1_peers[0]).wait()
        G2[b, pl.ds(g2_me, 1), :] = jnp.sum(G1[b], axis=0, keepdims=True)
        for dev_id in g2_peers:
            row = G2.at[b, pl.ds(g2_me, 1)]
            remote(row, row, g2_s.at[b], g2_r.at[b], dev_id).start()

        kept = []

        def regression(blk):
            prior3 = pack_quarters(*[PRI[b, blk, q] for q in range(4)])
            mean, dev, var = stats(prior3)
            used = META[blk, 4 + b : 5 + b]
            anom = dev * used
            innov = (META[blk, b : b + 1] - mean) * used
            kept.append((anom, innov, var))
            regress = anom / ((MEM - 1) * (var + EPS))
            hi = regress.astype(BF16).astype(F32)
            lo = regress - hi
            for t in range(3):
                cut = slice(t * LANES, (t + 1) * LANES)
                tall = jnp.concatenate([hi[:, cut], lo[:, cut], hi[:, cut], jnp.zeros((16, LANES), F32)], axis=0)
                RT[blk, cut, :] = tall.T.astype(BF16)

        def first_product(grp):
            for l in range(LEV):
                for c4 in range(4):
                    half, ct = c4 // 2, c4 % 2
                    blk = 0 if grp == 0 else 1 + half
                    cols = slice(c4 * 256, c4 * 256 + 256)
                    coef = jnp.dot(RT[blk], SPC[l, :, cols], preferred_element_type=F32)
                    hi, lo = split(coef * LOC[half, grp, :, ct * 256 : ct * 256 + 256])
                    ZH[l, grp * CAP : (grp + 1) * CAP, cols] = hi
                    ZL[l, grp * CAP : (grp + 1) * CAP, cols] = lo

        regression(0)
        first_product(0)
        if b == 0:
            for c in meta_copies:
                c.wait()
            build_gather(1)
        for side in range(2):
            for q in range(4):
                remote(PRI.at[b, 0, q], PRI.at[b, 1 + side, q], ha_s.at[b, side, q], ha_r.at[b, side, q],
                       {"col": right, "lev": j}).wait_recv()
        regression(1)
        regression(2)
        first_product(1)

        all15 = G2.at[b, pl.ds(0, 15)]
        remote(all15, all15, g2_s.at[b], g2_r.at[b], g2_peers[0]).wait()
        sums = jnp.sum(G2[b], axis=0, keepdims=True)
        inflation = sums[:, 0:1] / sums[:, 64:65]
        root = jnp.sqrt(inflation)
        for blk in range(3):
            anom, innov, var = kept[blk]
            noise = META[blk, 2 + b : 3 + b]
            v = inflation * var
            tot = v + noise
            shift = v * innov / tot + ((jnp.sqrt(noise / tot) - 1.0) * root) * anom
            hi, lo = split(shift)
            cut = slice(0, CAP) if blk == 0 else slice(CAP, 2 * CAP)
            for half in ((0, 1) if blk == 0 else (blk - 1,)):
                SC[half, 0:MEM, cut] = hi
                SC[half, MEM : 2 * MEM, cut] = lo

        target = X if b + 1 < BATCHES else OUT

        for l in range(LEV):
            for c4 in range(4):
                half = c4 // 2
                cols = slice(c4 * 256, c4 * 256 + 256)
                a = jnp.dot(SC[half], ZH[l, :, cols], preferred_element_type=F32)
                r = jnp.dot(SC[half, 0:MEM], ZL[l, :, cols], preferred_element_type=F32)
                centre = CEN[l, 0:1, cols]
                base = centre + root * (X[l, :, cols] - centre)
                target[l, :, cols] = base + (a[:MEM] + a[MEM:] + r)
            if b + 1 == BATCHES:
                c = pltpu.make_async_copy(OUT.at[l], out.at[l], out_sem.at[l])
                c.start()
                stores.append(c)

        if b + 1 < BATCHES:
            partial_priors(b + 1)

    for c in stores:
        c.wait()
    for c in pending:
        c.wait_send()


def hand_over(src, dst, buf, in_sem, out_sem):
    ins = [pltpu.make_async_copy(src.at[l], buf.at[l], in_sem.at[l]) for l in range(LEV)]
    outs = [pltpu.make_async_copy(buf.at[l], dst.at[l], out_sem.at[l]) for l in range(LEV)]
    for c in ins:
        c.start()
    for c, o in zip(ins, outs):
        c.wait()
        o.start()
    for o in outs:
        o.wait()


def shards(state, obs_col, obs_count, obs_value, obs_var, horiz_weight, vert_weight):
    dma = pltpu.SemaphoreType.DMA
    result = pl.pallas_call(
        kernel,
        name="window",
        out_shape=jax.ShapeDtypeStruct((LEV, MEM, COLS), F32),
        in_specs=[pl.BlockSpec(memory_space=pltpu.HBM)] * 7,
        out_specs=pl.BlockSpec(memory_space=pl.ANY),
        scratch_shapes=[
            pltpu.VMEM((3, BATCHES, CAP), jnp.int32),
            pltpu.VMEM((1, BATCHES), jnp.int32),
            pltpu.VMEM((BATCHES, CAP), F32),
            pltpu.VMEM((BATCHES, CAP), F32),
            pltpu.VMEM((BATCHES, 4, CAP), F32),
            pltpu.VMEM((LEV, BATCHES, CAP), F32),
            pltpu.VMEM((LEV, MEM, COLS), F32),
            pltpu.VMEM((LEV, MEM, COLS), F32),
            pltpu.VMEM((LEV, 8, COLS), F32),
            pltpu.VMEM((LEV, 256, COLS), BF16),
            pltpu.VMEM((2 * LEV * MEM, COLS), BF16),
            pltpu.VMEM((BATCHES, COLS, 4 * LANES), BF16),
            pltpu.VMEM((BATCHES, COLS, 4 * LANES), BF16),
            pltpu.VMEM((2, 2, CAP, HALF), F32),
            pltpu.VMEM((CAP, LANES), F32),
            pltpu.VMEM((3, CAP, 256), BF16),
            pltpu.VMEM((2, 2 * MEM, 2 * CAP), BF16),
            pltpu.VMEM((LEV, 2 * CAP, COLS), BF16),
            pltpu.VMEM((LEV, 2 * CAP, COLS), BF16),
            pltpu.VMEM((4, 8, LANES), F32),
            pltpu.VMEM((3, 8, CAP), F32),
            pltpu.VMEM((BATCHES, 4, MEM, LANES), F32),
            pltpu.VMEM((BATCHES, 3, MEM, LANES), F32),
            pltpu.VMEM((BATCHES, 3, 4, MEM, LANES), F32),
            pltpu.VMEM((BATCHES, 16, LANES), F32),
            pltpu.VMEM((BATCHES, 16, LANES), F32),
            dma((9,)),
            dma((LEV,)),
            dma((2,)), dma((2,)),
            dma((BATCHES, 3)), dma((BATCHES, 3)),
            dma((BATCHES, 3)), dma((BATCHES, 3)),
            dma((BATCHES, 2, 4)), dma((BATCHES, 2, 4)),
            dma((BATCHES,)), dma((BATCHES,)),
            dma((BATCHES,)), dma((BATCHES,)),
        ],
        compiler_params=pltpu.CompilerParams(
            collective_id=0, has_side_effects=True, vmem_limit_bytes=56 * 1024 * 1024
        ),
    )(
        state, obs_col, obs_count.T, obs_value, obs_var, horiz_weight, jnp.transpose(vert_weight, (1, 0, 2))
    )
    return pl.pallas_call(
        hand_over,
        name="hand_over",
        out_shape=jax.ShapeDtypeStruct((LEV, MEM, COLS), F32),
        in_specs=[pl.BlockSpec(memory_space=pl.ANY)],
        out_specs=pl.BlockSpec(memory_space=pl.ANY),
        scratch_shapes=[pltpu.VMEM((LEV, MEM, COLS), F32), dma((LEV,)), dma((LEV,))],
        compiler_params=pltpu.CompilerParams(vmem_limit_bytes=56 * 1024 * 1024),
    )(result)


def solution(mesh):
    placed = (
        P("lev", None, "col"),
        P(),
        P(None, "col"),
        P(None, "col"),
        P(None, "col"),
        P(None, None, "col"),
        P(None, "lev", "col"),
    )
    return jax.shard_map(
        shards, mesh=mesh, in_specs=placed, out_specs=P("lev", None, "col"), check_vma=False
    )
```

```python
import functools
import jax
import jax.numpy as jnp
from jax import lax
from jax.experimental import pallas as pl
from jax.experimental.pallas import tpu as pltpu
from jax.sharding import PartitionSpec as P

MESH = pl.DeviceIdType.MESH
F32 = jnp.float32
BF16 = jnp.bfloat16

BATCHES = 2
LEV = 5
MEM = 80
COLS = 1024
CAP = 384
QUART = 96
FOLD = 64
LANES = 128
HALF = 512
NZ = 8
NY = 4
NLEV = 4
EPS = 1e-06


def split(x):
    hi = x.astype(BF16)
    return hi, (x - hi.astype(F32)).astype(BF16)


def pad_quarters(x):
    return [
        (x if q == 0 else pltpu.roll(x, CAP - QUART * q, 1))[:, :LANES]
        for q in range(4)
    ]


def pack_quarters(q0, q1, q2, q3):
    lane = lax.broadcasted_iota(jnp.int32, q0.shape, 1)
    r1 = pltpu.roll(q1, 96, 1)
    r2 = pltpu.roll(q2, 64, 1)
    r3 = pltpu.roll(q3, 32, 1)
    return jnp.concatenate(
        [
            jnp.where(lane < 96, q0, r1),
            jnp.where(lane < 64, r1, r2),
            jnp.where(lane < 32, r2, r3),
        ],
        axis=1,
    )


def fold(x):
    lane = lax.broadcasted_iota(jnp.int32, (FOLD, LANES), 1)
    last = x[FOLD:]
    extra = [pltpu.roll(last, 96 - 32 * k, 1) for k in range(3)] + [jnp.zeros_like(last)]
    return jnp.where(lane < QUART, x[:FOLD], jnp.concatenate(extra, axis=0))


def unfold(p):
    lane = lax.broadcasted_iota(jnp.int32, (MEM - FOLD, LANES), 1)
    r = [pltpu.roll(p[16 * k : 16 * k + 16], 32 + 32 * k, 1) for k in range(3)]
    last = jnp.where(lane < 32, r[0], jnp.where(lane < 64, r[1], r[2]))
    return jnp.concatenate([p, last], axis=0)


def taper(d):
    u = 1.0 / 256.0
    near = ((-0.25 * u**5) * d + 0.5 * u**4) * d + 0.625 * u**3
    near = (near * d - (5.0 / 3.0) * u**2) * (d * d) + 1.0
    t = jnp.maximum(512.0 - d, 0.0)
    t2 = t * t
    far = (t2 * t2) * ((u**5 / 12.0) * d + u**4 / 6.0 - (u**3 / 24.0) * pl.reciprocal(d))
    return jnp.where(d <= 256.0, near, far)


def remote(src, dst, send, recv, dev):
    return pltpu.make_async_remote_copy(
        src_ref=src, dst_ref=dst, send_sem=send, recv_sem=recv,
        device_id=dev, device_id_type=MESH,
    )


def kernel(
    state, obs_col, obs_count, obs_value, obs_var, hw_in, vw_in, out,
    OCOL, OCNT, OVAL, OVAR, hw, vw, OUT, X, CEN, SPC, XHL, HH, HL, LOC, PT, RT, SC, ZH, ZL, MV, META, PART, RSB, PRI, G1, G2,
    in_sem, out_sem, meta_s, meta_r, rs_s, rs_r, ag_s, ag_r, ha_s, ha_r, g1_s, g1_r, g2_s, g2_r,
):
    i = lax.axis_index("col")
    j = lax.axis_index("lev")
    core = lax.rem(i, 2)
    z = lax.rem(i // 2, NZ)
    y = i // (2 * NZ)
    left = lax.rem(i + 63, 64)
    right = lax.rem(i + 1, 64)
    lev_peers = [lax.rem(j + d, NLEV) for d in range(NLEV)]
    g1_peers = [
        {"col": lax.rem(y + dy, NY) * 16 + z * 2 + core, "lev": lax.rem(j + dl, NLEV)}
        for dl in (2, 1, 3, 0) for dy in (2, 1, 3, 0) if dl or dy
    ]
    g2_peers = [
        {"col": y * 16 + lax.rem(z + dz, NZ) * 2 + lax.rem(core + dc, 2), "lev": j}
        for dz in (4, 3, 5, 2, 6, 1, 7, 0) for dc in (1, 0) if dz or dc
    ]
    g1_me = j * NY + y
    g2_me = z * 2 + core

    blocks = (i, left, right)
    loads = [
        pltpu.make_async_copy(obs_col.at[:, pl.ds(pl.multiple_of(b * CAP, CAP), CAP)], OCOL.at[n], in_sem.at[n])
        for n, b in enumerate(blocks)
    ]
    for n, (src, dst) in enumerate(
        ((obs_count, OCNT), (obs_value, OVAL), (obs_var, OVAR), (hw_in, hw), (vw_in, vw))
    ):
        loads.append(pltpu.make_async_copy(src, dst, in_sem.at[3 + n]))
    load_state = pltpu.make_async_copy(state, X, in_sem.at[8])
    for c in loads + [load_state]:
        c.start()
    barrier = pltpu.get_barrier_semaphore()
    partners = g1_peers + g2_peers + [{"col": left, "lev": j}, {"col": right, "lev": j}]
    for dev in partners:
        pl.semaphore_signal(barrier, inc=1, device_id=dev, device_id_type=MESH)
    for c in loads:
        c.wait()

    starts = [OCOL[n] for n in range(3)]
    lane384 = lax.broadcasted_iota(jnp.int32, (1, CAP), 1)
    use = [(lane384 < OCNT[0:1, b : b + 1]).astype(F32) for b in range(BATCHES)]
    def build_gather(b):
        lane = lax.broadcasted_iota(jnp.int32, (1, LANES), 1)
        valid = lane < QUART
        st = pad_quarters(starts[0] - i * COLS)
        h4 = pad_quarters(hw[b])
        start = jnp.concatenate([s[b : b + 1] for s in st], axis=1)
        w = jnp.concatenate([jnp.where(valid, h, 0.0) for h in h4], axis=1)

        @pl.loop(0, COLS // 32)
        def _(k):
            rows = pl.ds(pl.multiple_of(k * 32, 32), 32)
            t = lax.broadcasted_iota(jnp.int32, (32, 4 * LANES), 0) + (k * 32 - start)
            m = jnp.zeros((32, 4 * LANES), F32)
            for n in range(4):
                m = jnp.where(t == n, w[n : n + 1], m)
            HH[b, rows, :], HL[b, rows, :] = split(m)

    def build_taper(b, grp):
        for half in range(2):
            blk = 0 if grp == 0 else 1 + half

            @pl.loop(0, CAP // 192)
            def _(k):
                rows = pl.ds(pl.multiple_of(k * 192, 192), 192)
                p = PT[rows, 2 * blk + b : 2 * blk + b + 1]
                c = (lax.broadcasted_iota(jnp.int32, (192, HALF), 1) + half * HALF).astype(F32)
                LOC[half, grp, rows, :] = taper(jnp.abs(p - c))

    def split_state(l, cols, x):
        XHL[l * MEM : (l + 1) * MEM, cols], XHL[(LEV + l) * MEM : (LEV + l + 1) * MEM, cols] = split(x)

    def partial_priors(b):
        v4 = pad_quarters(vw[:, b, :])
        for n in range(2):
            cols = slice(n * 256, n * 256 + 256)
            a = jnp.dot(XHL[...], HH[b, :, cols], preferred_element_type=F32)
            r = jnp.dot(XHL[: LEV * MEM], HL[b, :, cols], preferred_element_type=F32)
            v = jnp.concatenate([v4[2 * n], v4[2 * n + 1]], axis=1)
            total = None
            for l in range(LEV):
                term = a[l * MEM : (l + 1) * MEM] + a[(LEV + l) * MEM : (LEV + l + 1) * MEM]
                term = (term + r[l * MEM : (l + 1) * MEM]) * v[l : l + 1]
                total = term if total is None else total + term
            PART[b, 2 * n] = fold(total[:, :LANES])
            PART[b, 2 * n + 1] = fold(total[:, LANES:])

    def prepare_spread():
        @pl.loop(0, LEV)
        def _(l):
            x = X[l]
            centre = jnp.mean(x, axis=0, keepdims=True)
            CEN[l] = jnp.broadcast_to(centre, (8, COLS))
            hi, lo = split(x - centre)
            SPC[l, 0:MEM] = hi
            SPC[l, MEM : 2 * MEM] = hi
            SPC[l, 2 * MEM : 3 * MEM] = lo
            SPC[l, 3 * MEM :] = jnp.zeros((16, COLS), BF16)

    def stats(prior):
        mean = jnp.sum(prior, axis=0, keepdims=True) / MEM
        dev = prior - mean
        var = jnp.sum(dev * dev, axis=0, keepdims=True) / (MEM - 1)
        return mean, dev, var

    build_gather(0)
    load_state.wait()
    for l in range(LEV):
        split_state(l, slice(0, COLS), X[l])
    partial_priors(0)
    pl.semaphore_wait(barrier, len(partners))

    meta_copies = [
        remote(META.at[0], META.at[1], meta_s.at[0], meta_r.at[0], {"col": right, "lev": j}),
        remote(META.at[0], META.at[2], meta_s.at[1], meta_r.at[1], {"col": left, "lev": j}),
    ]
    pending, stores = [], []

    for b in range(BATCHES):
        copies = []
        for d in (2, 1, 3):
            c = remote(PART.at[b, lev_peers[d]], RSB.at[b, d - 1], rs_s.at[b, d - 1], rs_r.at[b, d - 1],
                       {"col": i, "lev": lev_peers[d]})
            c.start()
            copies.append(c)
        if b == 0:
            META[0] = jnp.concatenate(
                [OVAL[...], OVAR[...], use[0], use[1], jnp.zeros((2, CAP), F32)], axis=0
            )
            MV[...] = jnp.stack(pad_quarters(META[0]))
            rel = [
                (starts[0] - i * COLS).astype(F32),
                (starts[1] - left * COLS - COLS).astype(F32),
                (starts[2] - right * COLS + COLS).astype(F32),
            ]
            PT[...] = jnp.concatenate(rel + [jnp.zeros((LANES - 6, CAP), F32)], axis=0).T
            for c in meta_copies:
                c.start()
        build_taper(b, 0)
        prepare_spread()
        for c in copies:
            c.wait_recv()
        pending += copies
        prior = PART[b, j] + (RSB[b, 0] + RSB[b, 1] + RSB[b, 2])
        PRI[b, 0, j] = prior

        mean, dev, var = stats(unfold(prior))
        lane = lax.broadcasted_iota(jnp.int32, (1, LANES), 1)
        value = MV[j, b : b + 1]
        noise = MV[j, 2 + b : 3 + b]
        used = jnp.where(lane < QUART, MV[j, 4 + b : 5 + b], 0.0)
        innov = (value - mean) * used
        misfit = jnp.sum(innov * innov, axis=1, keepdims=True)
        expected = jnp.sum(used * (var + noise), axis=1, keepdims=True)
        G1[b, pl.ds(g1_me, 1), :] = jnp.where(lane < 64, misfit, expected)
        for dev_id in g1_peers:
            row = G1.at[b, pl.ds(g1_me, 1)]
            remote(row, row, g1_s.at[b], g1_r.at[b], dev_id).start()
        def forward(q):
            made = [
                remote(PRI.at[b, 0, q], PRI.at[b, 1, q], ha_s.at[b, 0, q], ha_r.at[b, 0, q],
                       {"col": right, "lev": j}),
                remote(PRI.at[b, 0, q], PRI.at[b, 2, q], ha_s.at[b, 1, q], ha_r.at[b, 1, q],
                       {"col": left, "lev": j}),
            ]
            for c in made:
                c.start()
            pending.extend(made)

        gathers = []
        for d in (1, 3, 2):
            c = remote(PRI.at[b, 0, j], PRI.at[b, 0, j], ag_s.at[b, d - 1], ag_r.at[b, d - 1],
                       {"col": i, "lev": lev_peers[d]})
            c.start()
            gathers.append((d, c))
        forward(j)
        build_taper(b, 1)
        if b == 0:
            build_gather(1)
        for d, c in gathers:
            c.wait_recv()
            forward(lax.rem(j + NLEV - d, NLEV))
        pending += [c for _, c in gathers]

        all15 = G1.at[b, pl.ds(0, 15)]
        remote(all15, all15, g1_s.at[b], g1_r.at[b], g1_peers[0]).wait()
        G2[b, pl.ds(g2_me, 1), :] = jnp.sum(G1[b], axis=0, keepdims=True)
        for dev_id in g2_peers:
            row = G2.at[b, pl.ds(g2_me, 1)]
            remote(row, row, g2_s.at[b], g2_r.at[b], dev_id).start()

        kept = []

        def regression(blk):
            prior3 = pack_quarters(*[unfold(PRI[b, blk, q]) for q in range(4)])
            mean, dev, var = stats(prior3)
            used = META[blk, 4 + b : 5 + b]
            anom = dev * used
            innov = (META[blk, b : b + 1] - mean) * used
            kept.append((anom, innov, var))
            regress = anom / ((MEM - 1) * (var + EPS))
            hi = regress.astype(BF16).astype(F32)
            lo = regress - hi
            for t in range(3):
                cut = slice(t * LANES, (t + 1) * LANES)
                tall = jnp.concatenate([hi[:, cut], lo[:, cut], hi[:, cut], jnp.zeros((16, LANES), F32)], axis=0)
                RT[blk, cut, :] = tall.T.astype(BF16)

        def first_product(grp, halves=(0, 1)):
            for l in range(LEV):
                for c4 in range(4):
                    half, ct = c4 // 2, c4 % 2
                    if half not in halves:
                        continue
                    blk = 0 if grp == 0 else 1 + half
                    cols = slice(c4 * 256, c4 * 256 + 256)
                    coef = jnp.dot(RT[blk], SPC[l, :, cols], preferred_element_type=F32)
                    hi, lo = split(coef * LOC[half, grp, :, ct * 256 : ct * 256 + 256])
                    ZH[l, grp * CAP : (grp + 1) * CAP, cols] = hi
                    ZL[l, grp * CAP : (grp + 1) * CAP, cols] = lo

        regression(0)
        first_product(0)
        if b == 0:
            for c in meta_copies:
                c.wait()
        for side in range(2):
            for q in range(4):
                remote(PRI.at[b, 0, q], PRI.at[b, 1 + side, q], ha_s.at[b, side, q], ha_r.at[b, side, q],
                       {"col": right, "lev": j}).wait_recv()
            regression(1 + side)
            first_product(1, (side,))

        all15 = G2.at[b, pl.ds(0, 15)]
        remote(all15, all15, g2_s.at[b], g2_r.at[b], g2_peers[0]).wait()
        sums = jnp.sum(G2[b], axis=0, keepdims=True)
        inflation = sums[:, 0:1] / sums[:, 64:65]
        root = jnp.sqrt(inflation)
        for blk in range(3):
            anom, innov, var = kept[blk]
            noise = META[blk, 2 + b : 3 + b]
            v = inflation * var
            tot = v + noise
            shift = v * innov / tot + ((jnp.sqrt(noise / tot) - 1.0) * root) * anom
            hi, lo = split(shift)
            cut = slice(0, CAP) if blk == 0 else slice(CAP, 2 * CAP)
            for half in ((0, 1) if blk == 0 else (blk - 1,)):
                SC[half, 0:MEM, cut] = hi
                SC[half, MEM : 2 * MEM, cut] = lo

        target = X if b + 1 < BATCHES else OUT

        for l in range(LEV):
            for c4 in range(4):
                half = c4 // 2
                cols = slice(c4 * 256, c4 * 256 + 256)
                a = jnp.dot(SC[half], ZH[l, :, cols], preferred_element_type=F32)
                r = jnp.dot(SC[half, 0:MEM], ZL[l, :, cols], preferred_element_type=F32)
                centre = CEN[l, 0:1, cols]
                base = centre + root * (X[l, :, cols] - centre)
                new = base + (a[:MEM] + a[MEM:] + r)
                target[l, :, cols] = new
                if b + 1 < BATCHES:
                    split_state(l, cols, new)
            if b + 1 == BATCHES:
                c = pltpu.make_async_copy(OUT.at[l], out.at[l], out_sem.at[l])
                c.start()
                stores.append(c)

        if b + 1 < BATCHES:
            partial_priors(b + 1)

    for c in stores:
        c.wait()
    for c in pending:
        c.wait_send()


def hand_over(src, dst, buf, in_sem, out_sem):
    ins = [pltpu.make_async_copy(src.at[l], buf.at[l], in_sem.at[l]) for l in range(LEV)]
    outs = [pltpu.make_async_copy(buf.at[l], dst.at[l], out_sem.at[l]) for l in range(LEV)]
    for c in ins:
        c.start()
    for c, o in zip(ins, outs):
        c.wait()
        o.start()
    for o in outs:
        o.wait()


def shards(state, obs_col, obs_count, obs_value, obs_var, horiz_weight, vert_weight):
    dma = pltpu.SemaphoreType.DMA
    result = pl.pallas_call(
        kernel,
        name="window",
        out_shape=jax.ShapeDtypeStruct((LEV, MEM, COLS), F32),
        in_specs=[pl.BlockSpec(memory_space=pltpu.HBM)] * 7,
        out_specs=pl.BlockSpec(memory_space=pl.ANY),
        scratch_shapes=[
            pltpu.VMEM((3, BATCHES, CAP), jnp.int32),
            pltpu.VMEM((1, BATCHES), jnp.int32),
            pltpu.VMEM((BATCHES, CAP), F32),
            pltpu.VMEM((BATCHES, CAP), F32),
            pltpu.VMEM((BATCHES, 4, CAP), F32),
            pltpu.VMEM((LEV, BATCHES, CAP), F32),
            pltpu.VMEM((LEV, MEM, COLS), F32),
            pltpu.VMEM((LEV, MEM, COLS), F32),
            pltpu.VMEM((LEV, 8, COLS), F32),
            pltpu.VMEM((LEV, 256, COLS), BF16),
            pltpu.VMEM((2 * LEV * MEM, COLS), BF16),
            pltpu.VMEM((BATCHES, COLS, 4 * LANES), BF16),
            pltpu.VMEM((BATCHES, COLS, 4 * LANES), BF16),
            pltpu.VMEM((2, 2, CAP, HALF), F32),
            pltpu.VMEM((CAP, LANES), F32),
            pltpu.VMEM((3, CAP, 256), BF16),
            pltpu.VMEM((2, 2 * MEM, 2 * CAP), BF16),
            pltpu.VMEM((LEV, 2 * CAP, COLS), BF16),
            pltpu.VMEM((LEV, 2 * CAP, COLS), BF16),
            pltpu.VMEM((4, 8, LANES), F32),
            pltpu.VMEM((3, 8, CAP), F32),
            pltpu.VMEM((BATCHES, 4, FOLD, LANES), F32),
            pltpu.VMEM((BATCHES, 3, FOLD, LANES), F32),
            pltpu.VMEM((BATCHES, 3, 4, FOLD, LANES), F32),
            pltpu.VMEM((BATCHES, 16, LANES), F32),
            pltpu.VMEM((BATCHES, 16, LANES), F32),
            dma((9,)),
            dma((LEV,)),
            dma((2,)), dma((2,)),
            dma((BATCHES, 3)), dma((BATCHES, 3)),
            dma((BATCHES, 3)), dma((BATCHES, 3)),
            dma((BATCHES, 2, 4)), dma((BATCHES, 2, 4)),
            dma((BATCHES,)), dma((BATCHES,)),
            dma((BATCHES,)), dma((BATCHES,)),
        ],
        compiler_params=pltpu.CompilerParams(
            collective_id=0, has_side_effects=True, vmem_limit_bytes=56 * 1024 * 1024
        ),
    )(
        state, obs_col, obs_count.T, obs_value, obs_var, horiz_weight, jnp.transpose(vert_weight, (1, 0, 2))
    )
    return pl.pallas_call(
        hand_over,
        name="hand_over",
        out_shape=jax.ShapeDtypeStruct((LEV, MEM, COLS), F32),
        in_specs=[pl.BlockSpec(memory_space=pl.ANY)],
        out_specs=pl.BlockSpec(memory_space=pl.ANY),
        scratch_shapes=[pltpu.VMEM((LEV, MEM, COLS), F32), dma((LEV,)), dma((LEV,))],
        compiler_params=pltpu.CompilerParams(vmem_limit_bytes=56 * 1024 * 1024),
    )(result)


def solution(mesh):
    placed = (
        P("lev", None, "col"),
        P(),
        P(None, "col"),
        P(None, "col"),
        P(None, "col"),
        P(None, None, "col"),
        P(None, "lev", "col"),
    )
    return jax.shard_map(
        shards, mesh=mesh, in_specs=placed, out_specs=P("lev", None, "col"), check_vma=False
    )
```

```python
import functools
import jax
import jax.numpy as jnp
from jax import lax
from jax.experimental import pallas as pl
from jax.experimental.pallas import tpu as pltpu
from jax.sharding import PartitionSpec as P

MESH = pl.DeviceIdType.MESH
F32 = jnp.float32
BF16 = jnp.bfloat16

BATCHES = 2
LEV = 5
MEM = 80
COLS = 1024
CAP = 384
QUART = 96
FOLD = 64
LANES = 128
HALF = 512
NZ = 8
NY = 4
NLEV = 4
EPS = 1e-06


def split(x):
    hi = x.astype(BF16)
    return hi, (x - hi.astype(F32)).astype(BF16)


def pad_quarters(x):
    return [
        (x if q == 0 else pltpu.roll(x, CAP - QUART * q, 1))[:, :LANES]
        for q in range(4)
    ]


def pack_quarters(q0, q1, q2, q3):
    lane = lax.broadcasted_iota(jnp.int32, q0.shape, 1)
    r1 = pltpu.roll(q1, 96, 1)
    r2 = pltpu.roll(q2, 64, 1)
    r3 = pltpu.roll(q3, 32, 1)
    return jnp.concatenate(
        [
            jnp.where(lane < 96, q0, r1),
            jnp.where(lane < 64, r1, r2),
            jnp.where(lane < 32, r2, r3),
        ],
        axis=1,
    )


def fold(x):
    lane = lax.broadcasted_iota(jnp.int32, (FOLD, LANES), 1)
    last = x[FOLD:]
    extra = [pltpu.roll(last, 96 - 32 * k, 1) for k in range(3)] + [jnp.zeros_like(last)]
    return jnp.where(lane < QUART, x[:FOLD], jnp.concatenate(extra, axis=0))


def unfold(p):
    lane = lax.broadcasted_iota(jnp.int32, (MEM - FOLD, LANES), 1)
    r = [pltpu.roll(p[16 * k : 16 * k + 16], 32 + 32 * k, 1) for k in range(3)]
    last = jnp.where(lane < 32, r[0], jnp.where(lane < 64, r[1], r[2]))
    return jnp.concatenate([p, last], axis=0)


def taper(d):
    u = 1.0 / 256.0
    near = ((-0.25 * u**5) * d + 0.5 * u**4) * d + 0.625 * u**3
    near = (near * d - (5.0 / 3.0) * u**2) * (d * d) + 1.0
    t = jnp.maximum(512.0 - d, 0.0)
    t2 = t * t
    far = (t2 * t2) * ((u**5 / 12.0) * d + u**4 / 6.0 - (u**3 / 24.0) * pl.reciprocal(d))
    return jnp.where(d <= 256.0, near, far)


def remote(src, dst, send, recv, dev):
    return pltpu.make_async_remote_copy(
        src_ref=src, dst_ref=dst, send_sem=send, recv_sem=recv,
        device_id=dev, device_id_type=MESH,
    )


def kernel(
    state, obs_col, obs_count, obs_value, obs_var, hw_in, vw_in, out,
    OCOL, OCNT, OVAL, OVAR, hw, vw, OUT, X, CEN, SPC, XHL, HH, HL, LOC, PT, RT, SC, ZH, ZL, MV, META, PART, RSB, PRI, G1, G2,
    in_sem, out_sem, meta_s, meta_r, rs_s, rs_r, ag_s, ag_r, ha_s, ha_r, g1_s, g1_r, g2_s, g2_r,
):
    i = lax.axis_index("col")
    j = lax.axis_index("lev")
    core = lax.rem(i, 2)
    z = lax.rem(i // 2, NZ)
    y = i // (2 * NZ)
    left = lax.rem(i + 63, 64)
    right = lax.rem(i + 1, 64)
    lev_peers = [lax.rem(j + d, NLEV) for d in range(NLEV)]
    g1_peers = [
        {"col": lax.rem(y + dy, NY) * 16 + z * 2 + core, "lev": lax.rem(j + dl, NLEV)}
        for dl in (2, 1, 3, 0) for dy in (2, 1, 3, 0) if dl or dy
    ]
    g2_peers = [
        {"col": y * 16 + lax.rem(z + dz, NZ) * 2 + lax.rem(core + dc, 2), "lev": j}
        for dz in (4, 3, 5, 2, 6, 1, 7, 0) for dc in (1, 0) if dz or dc
    ]
    g1_me = j * NY + y
    g2_me = z * 2 + core

    blocks = (i, left, right)
    loads = [
        pltpu.make_async_copy(obs_col.at[:, pl.ds(pl.multiple_of(b * CAP, CAP), CAP)], OCOL.at[n], in_sem.at[n])
        for n, b in enumerate(blocks)
    ]
    for n, (src, dst) in enumerate(
        ((obs_count, OCNT), (obs_value, OVAL), (obs_var, OVAR), (hw_in, hw), (vw_in, vw))
    ):
        loads.append(pltpu.make_async_copy(src, dst, in_sem.at[3 + n]))
    load_state = pltpu.make_async_copy(state, X, in_sem.at[8])
    for c in loads + [load_state]:
        c.start()
    barrier = pltpu.get_barrier_semaphore()
    partners = g1_peers + g2_peers + [{"col": left, "lev": j}, {"col": right, "lev": j}]
    for dev in partners:
        pl.semaphore_signal(barrier, inc=1, device_id=dev, device_id_type=MESH)
    for c in loads:
        c.wait()

    starts = [OCOL[n] for n in range(3)]
    lane384 = lax.broadcasted_iota(jnp.int32, (1, CAP), 1)
    use = [(lane384 < OCNT[0:1, b : b + 1]).astype(F32) for b in range(BATCHES)]
    def build_gather(b):
        lane = lax.broadcasted_iota(jnp.int32, (1, LANES), 1)
        valid = lane < QUART
        st = pad_quarters(starts[0] - i * COLS)
        h4 = pad_quarters(hw[b])
        start = jnp.concatenate([s[b : b + 1] for s in st], axis=1)
        w = jnp.concatenate([jnp.where(valid, h, 0.0) for h in h4], axis=1)

        @pl.loop(0, COLS // 32)
        def _(k):
            rows = pl.ds(pl.multiple_of(k * 32, 32), 32)
            t = lax.broadcasted_iota(jnp.int32, (32, 4 * LANES), 0) + (k * 32 - start)
            m = jnp.zeros((32, 4 * LANES), F32)
            for n in range(4):
                m = jnp.where(t == n, w[n : n + 1], m)
            HH[b, rows, :], HL[b, rows, :] = split(m)

    def build_taper(b, grp):
        for half in range(2):
            blk = 0 if grp == 0 else 1 + half

            @pl.loop(0, CAP // 192)
            def _(k):
                rows = pl.ds(pl.multiple_of(k * 192, 192), 192)
                p = PT[rows, 2 * blk + b : 2 * blk + b + 1]
                c = (lax.broadcasted_iota(jnp.int32, (192, HALF), 1) + half * HALF).astype(F32)
                LOC[half, grp, rows, :] = taper(jnp.abs(p - c))

    def split_state(l, cols, x):
        XHL[l * MEM : (l + 1) * MEM, cols], XHL[(LEV + l) * MEM : (LEV + l + 1) * MEM, cols] = split(x)

    def partial_priors(b):
        v4 = pad_quarters(vw[:, b, :])
        for n in range(2):
            cols = slice(n * 256, n * 256 + 256)
            a = jnp.dot(XHL[...], HH[b, :, cols], preferred_element_type=F32)
            r = jnp.dot(XHL[: LEV * MEM], HL[b, :, cols], preferred_element_type=F32)
            v = jnp.concatenate([v4[2 * n], v4[2 * n + 1]], axis=1)
            total = None
            for l in range(LEV):
                term = a[l * MEM : (l + 1) * MEM] + a[(LEV + l) * MEM : (LEV + l + 1) * MEM]
                term = (term + r[l * MEM : (l + 1) * MEM]) * v[l : l + 1]
                total = term if total is None else total + term
            PART[b, 2 * n] = fold(total[:, :LANES])
            PART[b, 2 * n + 1] = fold(total[:, LANES:])

    def prepare_spread():
        @pl.loop(0, LEV)
        def _(l):
            x = X[l]
            centre = jnp.mean(x, axis=0, keepdims=True)
            CEN[l] = jnp.broadcast_to(centre, (8, COLS))
            hi, lo = split(x - centre)
            SPC[l, 0:MEM] = hi
            SPC[l, MEM : 2 * MEM] = hi
            SPC[l, 2 * MEM : 3 * MEM] = lo
            SPC[l, 3 * MEM :] = jnp.zeros((16, COLS), BF16)

    def stats(prior):
        mean = jnp.sum(prior, axis=0, keepdims=True) / MEM
        dev = prior - mean
        var = jnp.sum(dev * dev, axis=0, keepdims=True) / (MEM - 1)
        return mean, dev, var

    build_gather(0)
    load_state.wait()
    for l in range(LEV):
        split_state(l, slice(0, COLS), X[l])
    partial_priors(0)
    pl.semaphore_wait(barrier, len(partners))

    meta_copies = [
        remote(META.at[0], META.at[1], meta_s.at[0], meta_r.at[0], {"col": right, "lev": j}),
        remote(META.at[0], META.at[2], meta_s.at[1], meta_r.at[1], {"col": left, "lev": j}),
    ]
    pending, stores = [], []

    for b in range(BATCHES):
        copies = []
        for d in (2, 1, 3):
            c = remote(PART.at[b, lev_peers[d]], RSB.at[b, d - 1], rs_s.at[b, d - 1], rs_r.at[b, d - 1],
                       {"col": i, "lev": lev_peers[d]})
            c.start()
            copies.append(c)
        if b == 0:
            META[0] = jnp.concatenate(
                [OVAL[...], OVAR[...], use[0], use[1], jnp.zeros((2, CAP), F32)], axis=0
            )
            MV[...] = jnp.stack(pad_quarters(META[0]))
            rel = [
                (starts[0] - i * COLS).astype(F32),
                (starts[1] - left * COLS - COLS).astype(F32),
                (starts[2] - right * COLS + COLS).astype(F32),
            ]
            PT[...] = jnp.concatenate(rel + [jnp.zeros((LANES - 6, CAP), F32)], axis=0).T
            for c in meta_copies:
                c.start()
        build_taper(b, 0)
        prepare_spread()
        for c in copies:
            c.wait_recv()
        pending += copies
        prior = PART[b, j] + (RSB[b, 0] + RSB[b, 1] + RSB[b, 2])
        PRI[b, 0, j] = prior

        mean, dev, var = stats(unfold(prior))
        lane = lax.broadcasted_iota(jnp.int32, (1, LANES), 1)
        value = MV[j, b : b + 1]
        noise = MV[j, 2 + b : 3 + b]
        used = jnp.where(lane < QUART, MV[j, 4 + b : 5 + b], 0.0)
        innov = (value - mean) * used
        misfit = jnp.sum(innov * innov, axis=1, keepdims=True)
        expected = jnp.sum(used * (var + noise), axis=1, keepdims=True)
        G1[b, pl.ds(g1_me, 1), :] = jnp.where(lane < 64, misfit, expected)
        for dev_id in g1_peers:
            row = G1.at[b, pl.ds(g1_me, 1)]
            remote(row, row, g1_s.at[b], g1_r.at[b], dev_id).start()
        def forward(q):
            off = lax.rem(i + 63 + 2 * core, 64)
            on = i + 1 - 2 * core
            made = [
                remote(PRI.at[b, 0, q], PRI.at[b, 2 - core, q], ha_s.at[b, 1 - core, q], ha_r.at[b, 1 - core, q],
                       {"col": off, "lev": j}),
                remote(PRI.at[b, 0, q], PRI.at[b, 1 + core, q], ha_s.at[b, core, q], ha_r.at[b, core, q],
                       {"col": on, "lev": j}),
            ]
            for c in made:
                c.start()
            pending.extend(made)

        gathers = []
        for d in (1, 3, 2):
            c = remote(PRI.at[b, 0, j], PRI.at[b, 0, j], ag_s.at[b, d - 1], ag_r.at[b, d - 1],
                       {"col": i, "lev": lev_peers[d]})
            c.start()
            gathers.append((d, c))
        forward(j)
        build_taper(b, 1)
        if b == 0:
            build_gather(1)
        for d, c in gathers:
            c.wait_recv()
            forward(lax.rem(j + NLEV - d, NLEV))
        pending += [c for _, c in gathers]

        all15 = G1.at[b, pl.ds(0, 15)]
        remote(all15, all15, g1_s.at[b], g1_r.at[b], g1_peers[0]).wait()
        G2[b, pl.ds(g2_me, 1), :] = jnp.sum(G1[b], axis=0, keepdims=True)
        for dev_id in g2_peers:
            row = G2.at[b, pl.ds(g2_me, 1)]
            remote(row, row, g2_s.at[b], g2_r.at[b], dev_id).start()

        kept = []

        def regression(blk):
            prior3 = pack_quarters(*[unfold(PRI[b, blk, q]) for q in range(4)])
            mean, dev, var = stats(prior3)
            used = META[blk, 4 + b : 5 + b]
            anom = dev * used
            innov = (META[blk, b : b + 1] - mean) * used
            kept.append((blk, anom, innov, var))
            regress = anom / ((MEM - 1) * (var + EPS))
            hi = regress.astype(BF16).astype(F32)
            lo = regress - hi
            for t in range(3):
                cut = slice(t * LANES, (t + 1) * LANES)
                tall = jnp.concatenate([hi[:, cut], lo[:, cut], hi[:, cut], jnp.zeros((16, LANES), F32)], axis=0)
                RT[blk, cut, :] = tall.T.astype(BF16)

        def own_product():
            for l in range(LEV):
                for c4 in range(4):
                    half, ct = c4 // 2, c4 % 2
                    cols = slice(c4 * 256, c4 * 256 + 256)
                    coef = jnp.dot(RT[0], SPC[l, :, cols], preferred_element_type=F32)
                    hi, lo = split(coef * LOC[half, 0, :, ct * 256 : ct * 256 + 256])
                    ZH[l, 0:CAP, cols] = hi
                    ZL[l, 0:CAP, cols] = lo

        def side_product(side):
            for l in range(LEV):
                for ct in range(2):
                    cols = pl.ds(pl.multiple_of(side * HALF + ct * 256, 256), 256)
                    coef = jnp.dot(RT[1 + side], SPC[l, :, cols], preferred_element_type=F32)
                    hi, lo = split(coef * LOC[side, 1, :, ct * 256 : ct * 256 + 256])
                    ZH[l, CAP : 2 * CAP, cols] = hi
                    ZL[l, CAP : 2 * CAP, cols] = lo

        regression(0)
        own_product()
        if b == 0:
            for c in meta_copies:
                c.wait()
        for side in (1 - core, core):
            for q in range(4):
                remote(PRI.at[b, 0, q], PRI.at[b, 1 + side, q], ha_s.at[b, side, q], ha_r.at[b, side, q],
                       {"col": right, "lev": j}).wait_recv()
            regression(1 + side)
            side_product(side)

        all15 = G2.at[b, pl.ds(0, 15)]
        remote(all15, all15, g2_s.at[b], g2_r.at[b], g2_peers[0]).wait()
        sums = jnp.sum(G2[b], axis=0, keepdims=True)
        inflation = sums[:, 0:1] / sums[:, 64:65]
        root = jnp.sqrt(inflation)
        for n, (blk, anom, innov, var) in enumerate(kept):
            noise = META[blk, 2 + b : 3 + b]
            v = inflation * var
            tot = v + noise
            shift = v * innov / tot + ((jnp.sqrt(noise / tot) - 1.0) * root) * anom
            hi, lo = split(shift)
            cut = slice(0, CAP) if n == 0 else slice(CAP, 2 * CAP)
            for half in (0, 1) if n == 0 else (blk - 1,):
                SC[half, 0:MEM, cut] = hi
                SC[half, MEM : 2 * MEM, cut] = lo

        target = X if b + 1 < BATCHES else OUT

        for l in range(LEV):
            for c4 in range(4):
                half = c4 // 2
                cols = slice(c4 * 256, c4 * 256 + 256)
                a = jnp.dot(SC[half], ZH[l, :, cols], preferred_element_type=F32)
                r = jnp.dot(SC[half, 0:MEM], ZL[l, :, cols], preferred_element_type=F32)
                centre = CEN[l, 0:1, cols]
                base = centre + root * (X[l, :, cols] - centre)
                new = base + (a[:MEM] + a[MEM:] + r)
                target[l, :, cols] = new
                if b + 1 < BATCHES:
                    split_state(l, cols, new)
            if b + 1 == BATCHES:
                c = pltpu.make_async_copy(OUT.at[l], out.at[l], out_sem.at[l])
                c.start()
                stores.append(c)

        if b + 1 < BATCHES:
            partial_priors(b + 1)

    for c in stores:
        c.wait()
    for c in pending:
        c.wait_send()


def hand_over(src, dst, buf, in_sem, out_sem):
    ins = [pltpu.make_async_copy(src.at[l], buf.at[l], in_sem.at[l]) for l in range(LEV)]
    outs = [pltpu.make_async_copy(buf.at[l], dst.at[l], out_sem.at[l]) for l in range(LEV)]
    for c in ins:
        c.start()
    for c, o in zip(ins, outs):
        c.wait()
        o.start()
    for o in outs:
        o.wait()


def shards(state, obs_col, obs_count, obs_value, obs_var, horiz_weight, vert_weight):
    dma = pltpu.SemaphoreType.DMA
    result = pl.pallas_call(
        kernel,
        name="window",
        out_shape=jax.ShapeDtypeStruct((LEV, MEM, COLS), F32),
        in_specs=[pl.BlockSpec(memory_space=pltpu.HBM)] * 7,
        out_specs=pl.BlockSpec(memory_space=pl.ANY),
        scratch_shapes=[
            pltpu.VMEM((3, BATCHES, CAP), jnp.int32),
            pltpu.VMEM((1, BATCHES), jnp.int32),
            pltpu.VMEM((BATCHES, CAP), F32),
            pltpu.VMEM((BATCHES, CAP), F32),
            pltpu.VMEM((BATCHES, 4, CAP), F32),
            pltpu.VMEM((LEV, BATCHES, CAP), F32),
            pltpu.VMEM((LEV, MEM, COLS), F32),
            pltpu.VMEM((LEV, MEM, COLS), F32),
            pltpu.VMEM((LEV, 8, COLS), F32),
            pltpu.VMEM((LEV, 256, COLS), BF16),
            pltpu.VMEM((2 * LEV * MEM, COLS), BF16),
            pltpu.VMEM((BATCHES, COLS, 4 * LANES), BF16),
            pltpu.VMEM((BATCHES, COLS, 4 * LANES), BF16),
            pltpu.VMEM((2, 2, CAP, HALF), F32),
            pltpu.VMEM((CAP, LANES), F32),
            pltpu.VMEM((3, CAP, 256), BF16),
            pltpu.VMEM((2, 2 * MEM, 2 * CAP), BF16),
            pltpu.VMEM((LEV, 2 * CAP, COLS), BF16),
            pltpu.VMEM((LEV, 2 * CAP, COLS), BF16),
            pltpu.VMEM((4, 8, LANES), F32),
            pltpu.VMEM((3, 8, CAP), F32),
            pltpu.VMEM((BATCHES, 4, FOLD, LANES), F32),
            pltpu.VMEM((BATCHES, 3, FOLD, LANES), F32),
            pltpu.VMEM((BATCHES, 3, 4, FOLD, LANES), F32),
            pltpu.VMEM((BATCHES, 16, LANES), F32),
            pltpu.VMEM((BATCHES, 16, LANES), F32),
            dma((9,)),
            dma((LEV,)),
            dma((2,)), dma((2,)),
            dma((BATCHES, 3)), dma((BATCHES, 3)),
            dma((BATCHES, 3)), dma((BATCHES, 3)),
            dma((BATCHES, 2, 4)), dma((BATCHES, 2, 4)),
            dma((BATCHES,)), dma((BATCHES,)),
            dma((BATCHES,)), dma((BATCHES,)),
        ],
        compiler_params=pltpu.CompilerParams(
            collective_id=0, has_side_effects=True, vmem_limit_bytes=56 * 1024 * 1024
        ),
    )(
        state, obs_col, obs_count.T, obs_value, obs_var, horiz_weight, jnp.transpose(vert_weight, (1, 0, 2))
    )
    return pl.pallas_call(
        hand_over,
        name="hand_over",
        out_shape=jax.ShapeDtypeStruct((LEV, MEM, COLS), F32),
        in_specs=[pl.BlockSpec(memory_space=pl.ANY)],
        out_specs=pl.BlockSpec(memory_space=pl.ANY),
        scratch_shapes=[pltpu.VMEM((LEV, MEM, COLS), F32), dma((LEV,)), dma((LEV,))],
        compiler_params=pltpu.CompilerParams(vmem_limit_bytes=56 * 1024 * 1024),
    )(result)


def solution(mesh):
    placed = (
        P("lev", None, "col"),
        P(),
        P(None, "col"),
        P(None, "col"),
        P(None, "col"),
        P(None, None, "col"),
        P(None, "lev", "col"),
    )
    return jax.shard_map(
        shards, mesh=mesh, in_specs=placed, out_specs=P("lev", None, "col"), check_vma=False
    )
```
